32 devices in a mesh: dp: 8 (over z, core), ctx: 4 (over y, x).
Axes of the slice: x: 2, y: 2, z: 4, core: 2. Of those that a mesh axis runs over, the one named last changes fastest.
Arguments:
- hidden_in: bfloat16 [8, 1536, 896], P('dp', 'ctx'), may hold values from -6 to 6
- doc_start: int32 [8, 1536], P('dp', 'ctx'), may hold values from 0 to 1535, as said below
- cotangent: bfloat16 [8, 1536, 896], P('dp', 'ctx'), may hold values from -6 to 6
- attn_weight: bfloat16 [2048, 896], P(('dp', 'ctx'))
- gate_up: bfloat16 [9728, 896], P(('dp', 'ctx')), may hold values from -0.1875 to 0.1875
- down_weight: bfloat16 [4864, 896], P(('dp', 'ctx')), may hold values from -0.078125 to 0.078125
- gain_attn: bfloat16 [896], P('ctx'), may hold values from 0.25 to 1.75
- gain_mlp: bfloat16 [896], P('ctx'), may hold values from 0.25 to 1.75
- qkv_bias: bfloat16 [1152], P('ctx'), may hold values from -2 to 2
Outputs:
- layer_out: bfloat16 [8, 1536, 896], P('dp', 'ctx')
- input_grad: bfloat16 [8, 1536, 896], P('dp', 'ctx')
- attn_weight_grad: float32 [2048, 896], P(('dp', 'ctx'))
- gate_up_grad: float32 [9728, 896], P(('dp', 'ctx'))
- down_weight_grad: float32 [4864, 896], P(('dp', 'ctx'))
- gain_attn_grad: float32 [896], P('ctx')
- gain_mlp_grad: float32 [896], P('ctx')
- qkv_bias_grad: float32 [1152], P('ctx')
The draws below stay inside these ranges and needn't reach their ends.
Inputs may be any that keep to these rules, and one draw needn't show every extreme that they name: doc_start never exceeds the token's own index, never falls along a sequence, and each token either starts its document or has its predecessor's doc_start. In every sequence one document begins among the first 384 tokens and ends among the last 384; the others hold 200 to 2000 tokens, fewer where the sequence's ends or that document cut them.
All inputs are finite; a program needn't handle non-finite values.
Results may differ from the reference program's by a relative error of at most 0.014.
Values may be sent and summed in bfloat16 or wider, within the bound.
A program may use at most 192 MiB of HBM per device.

```python
import math
import jax
import jax.numpy as jnp
from jax import lax

D = 896
HEADS = 14
KVH = 2
HD = 64
FF = 4864
TOK_DEV = 384
MINDOC = 200
MAXDOC = 2000
KVD = 128
QKVD = 1152
ATTROWS = 2048
SEQ = 1536
SEQUENCES = 8


def draw_doc_start(key, part):
    key = jax.random.fold_in(key, 11)
    key_lens, key_first, key_last = jax.random.split(key, 3)
    pieces = SEQ // MINDOC + 2
    lengths = jax.random.randint(key_lens, (SEQUENCES, pieces), MINDOC, MAXDOC + 1)
    starts = jnp.cumsum(lengths, axis=1) - lengths
    first_start = jax.random.randint(key_first, (SEQUENCES, 1), 0, TOK_DEV)
    last_end = jax.random.randint(key_last, (SEQUENCES, 1), SEQ - TOK_DEV + 1, SEQ + 1)
    positions = jnp.arange(SEQ, dtype=jnp.int32)[None, :]
    regular = jnp.max(jnp.where(starts[:, None, :] <= positions[:, :, None], starts[:, None, :], 0), axis=2)
    inside = jnp.where(positions < last_end, first_start, jnp.maximum(regular, last_end))
    return jnp.where(positions < first_start, regular, inside).astype(jnp.int32)


def draw_attn_weight(key, part):
    key = jax.random.fold_in(key, 7)
    values = jax.random.normal(key, (ATTROWS, D), jnp.float32)
    row_ids = jnp.arange(ATTROWS)[:, None]
    scales = jnp.where(row_ids < QKVD, 1.0, 5.0) * D ** (-0.5)
    return (values * scales).astype(jnp.bfloat16)


def block_levels(stream_key, shape, shards, least, top_value):
    level, own = 1.0, jax.random.fold_in(stream_key, 6)
    for dim, parts in shards:
        draws = jnp.exp(jax.random.uniform(jax.random.fold_in(own, dim), (parts,), jnp.float32, least / len(shards), top_value / len(shards)))
        level = level * jnp.repeat(draws, shape[dim] // parts).reshape([-1 if axis == dim else 1 for axis in range(len(shape))])
    return level


def bell_draw(key, shape, scale, bound, cuts=(), held_as=jnp.bfloat16):
    array = scale * jax.random.normal(key, shape, jnp.float32)
    if cuts:
        array = array * block_levels(key, shape, cuts, -0.22, 0.18)
    return jnp.clip(array, -bound, bound).astype(held_as)


def setup_inputs(seed: int = 0) -> dict:
    streams_of = jax.random.split(jax.random.key(seed), 10)
    hidden_in = bell_draw(streams_of[0], (SEQUENCES, SEQ, D), 1.0, 6.0, ((0, 8), (1, 4)))
    doc_start = draw_doc_start(jax.random.fold_in(streams_of[9], 71), 0)
    cotangent = bell_draw(streams_of[2], (SEQUENCES, SEQ, D), 1.0, 6.0, ((0, 8), (1, 4)))
    attn_weight = draw_attn_weight(jax.random.fold_in(streams_of[9], 71), 0)
    gate_up = bell_draw(streams_of[4], (2 * FF, D), D ** -0.5, 0.1875, ((0, 32),))
    down_weight = bell_draw(streams_of[5], (FF, D), FF ** -0.5, 0.078125, ((0, 32),))
    gain_attn = jnp.clip(1.0 + 0.15 * jax.random.normal(streams_of[6], (D,), jnp.float32), 0.25, 1.75).astype(jnp.bfloat16)
    gain_mlp = jnp.clip(1.0 + 0.15 * jax.random.normal(streams_of[7], (D,), jnp.float32), 0.25, 1.75).astype(jnp.bfloat16)
    qkv_bias = bell_draw(streams_of[8], (QKVD,), 0.3, 2.0, ((0, 4),))
    return {"hidden_in": hidden_in, "doc_start": doc_start, "cotangent": cotangent, "attn_weight": attn_weight, "gate_up": gate_up, "down_weight": down_weight, "gain_attn": gain_attn, "gain_mlp": gain_mlp, "qkv_bias": qkv_bias}


epsilon = 1e-06
rope_base = 1000000.0
highest = lax.Precision.HIGHEST

@jax.custom_vjp
def low(v):
    return lax.optimization_barrier(v.astype(jnp.bfloat16)).astype(jnp.float32)

@jax.custom_vjp
def low_back(v):
    return v

def low_keep(v):
    return (low(v), None)

def low_pass(kept, grad):
    return (grad,)

def back_keep(v):
    return (v, None)

def back_low(kept, grad):
    return (low(grad),)
low.defvjp(low_keep, low_pass)
low_back.defvjp(back_keep, back_low)

def rotate(values, positions):
    half_dim = HD // 2
    frequency = rope_base ** (-jnp.arange(half_dim).astype(jnp.float32) * (2.0 / HD))
    angles = positions.astype(jnp.float32)[:, None] * frequency[None, :]
    cosine = jnp.cos(angles)[:, None, :]
    sine_part = jnp.sin(angles)[:, None, :]
    first_half = values[..., :half_dim]
    second_half = values[..., half_dim:]
    return jnp.concatenate([first_half * cosine - second_half * sine_part, second_half * cosine + first_half * sine_part], -1)

def rms_norm(values, gain_vec):
    factor = lax.rsqrt(lax.optimization_barrier(jnp.mean(values * values, -1, keepdims=True)) + epsilon)
    return values * factor * gain_vec

def attention(queries, key_vals, value_vals, starts):
    seq_len = queries.shape[0]
    groups = HEADS // KVH
    block_len = math.gcd(seq_len, 512)
    blocks = seq_len // block_len
    query_blocks = queries.reshape(blocks, block_len, KVH, groups, HD)
    start_blocks = starts.reshape(blocks, block_len)
    columns = jnp.arange(seq_len, dtype=jnp.int32)
    scaling = HD ** (-0.5)

    def one_block(inputs):
        query_block, start_block, block_idx = inputs
        row_ids = block_idx * block_len + jnp.arange(block_len, dtype=jnp.int32)
        raw_scores = jnp.einsum('qkgd,nkd->kgqn', query_block, key_vals, precision=highest) * scaling
        raw_scores = low_back(raw_scores)
        allowed = (columns[None, :] <= row_ids[:, None]) & (columns[None, :] >= start_block[:, None])
        masked = jnp.where(allowed, raw_scores, -1e+30)
        row_top = lax.optimization_barrier(jnp.max(masked, -1, keepdims=True))
        exp_terms = jnp.where(allowed, jnp.exp(masked - row_top), 0.0)
        prob_low = low(exp_terms / lax.optimization_barrier(jnp.sum(exp_terms, -1, keepdims=True)))
        mixed_block = jnp.einsum('kgqn,nkd->qkgd', prob_low, value_vals, precision=highest)
        return mixed_block.reshape(block_len, HEADS * HD)
    outputs = lax.map(jax.checkpoint(one_block), (query_blocks, start_blocks, jnp.arange(blocks, dtype=jnp.int32)))
    return outputs.reshape(seq_len, HEADS * HD)

def one_layer(stream, starts, attn_w, gate_w, down_w, gain_one, gain_two, bias_vec):
    seq_len = stream.shape[0]
    positions = jnp.arange(seq_len, dtype=jnp.int32) - starts
    normed_one = low(rms_norm(stream, gain_one))
    projected = low_back(jnp.dot(normed_one, attn_w[:QKVD].T, precision=highest) + bias_vec)
    queries = low(rotate(projected[:, :D].reshape(seq_len, HEADS, HD), positions))
    key_vals = low(rotate(projected[:, D:D + KVD].reshape(seq_len, KVH, HD), positions))
    value_vals = low(projected[:, D + KVD:].reshape(seq_len, KVH, HD))
    groups = HEADS // KVH
    mixed_out = attention(queries.reshape(seq_len, KVH, groups, HD), key_vals, value_vals, starts)
    mixed_out = low_back(low(mixed_out))
    residual = stream + low_back(jnp.dot(mixed_out, attn_w[QKVD:], precision=highest))
    normed_two = low(rms_norm(residual, gain_two))
    gate_up_act = low_back(jnp.dot(normed_two, gate_w.T, precision=highest))
    activated = low(jax.nn.silu(gate_up_act[:, :FF]) * gate_up_act[:, FF:])
    return residual + low_back(jnp.dot(activated, down_w, precision=highest))

def reference(hidden_in, doc_start, cotangent, attn_weight, gate_up, down_weight, gain_attn, gain_mlp, qkv_bias):
    params = (attn_weight.astype(jnp.float32), gate_up.astype(jnp.float32), down_weight.astype(jnp.float32), gain_attn.astype(jnp.float32), gain_mlp.astype(jnp.float32), qkv_bias.astype(jnp.float32))
    inputs = hidden_in.astype(jnp.float32)

    def forward(stream, attn_w, gate_w, down_w, gain_one, gain_two, bias_vec):

        def step_fn(seq_pair):
            return one_layer(seq_pair[0], seq_pair[1], attn_w, gate_w, down_w, gain_one, gain_two, bias_vec)
        return lax.map(jax.checkpoint(step_fn), (stream, doc_start))
    output, pullback = jax.vjp(forward, inputs, *params)
    all_grads = pullback(cotangent.astype(jnp.float32))
    return (output.astype(jnp.bfloat16), all_grads[0].astype(jnp.bfloat16), all_grads[1], all_grads[2], all_grads[3], all_grads[4], all_grads[5], all_grads[6])
```

```python
import math

import jax
import jax.numpy as jnp
from jax import lax
from jax.sharding import PartitionSpec as P

D = 896
HEADS = 14
KVH = 2
HD = 64
FF = 4864
KVD = 128
QKVD = 1152


epsilon = 1e-06
rope_base = 1000000.0
masked_value = -1e30


def rope_tables(positions):
    half_dim = HD // 2
    frequency = rope_base ** (-jnp.arange(half_dim).astype(jnp.float32) * (2.0 / HD))
    angles = positions.astype(jnp.float32)[:, None] * frequency[None, :]
    return (jnp.cos(angles)[:, None, :], jnp.sin(angles)[:, None, :])


def rotate(values, cosine, sine_part):
    half_dim = values.shape[-1] // 2
    first_half = values[..., :half_dim]
    second_half = values[..., half_dim:]
    return jnp.concatenate(
        [
            first_half * cosine - second_half * sine_part,
            second_half * cosine + first_half * sine_part,
        ],
        -1,
    )


def unrotate(grad_in, cosine, sine_part):
    half_dim = grad_in.shape[-1] // 2
    first_half = grad_in[..., :half_dim]
    second_half = grad_in[..., half_dim:]
    return jnp.concatenate(
        [
            first_half * cosine + second_half * sine_part,
            second_half * cosine - first_half * sine_part,
        ],
        -1,
    )


def norm_back(grad_out, values, factor, gain_vec):
    scaled = grad_out * gain_vec
    gain_grad = jnp.sum(grad_out * values * factor, 0)
    inner_mean = jnp.mean(scaled * values, -1, keepdims=True)
    return (gain_grad, factor * scaled - values * factor**3 * inner_mean)


def contract_rows(left_op, right_op):
    return lax.dot_general(
        left_op, right_op, (((0,), (0,)), ((), ())), preferred_element_type=jnp.float32
    )


def contract_cols(left_op, right_op):
    return lax.dot_general(
        left_op, right_op, (((1,), (1,)), ((), ())), preferred_element_type=jnp.float32
    )


def column_term(left_op, right_op):
    return contract_rows(left_op, right_op)


def index_bits(axis_name):
    count = (lax.axis_size(axis_name) - 1).bit_length()
    return [(axis_name, bit) for bit in reversed(range(count))]


def split_bits(partial, bits):
    rows = partial.shape[0] >> len(bits)
    return partial.reshape([2] * len(bits) + [rows, partial.shape[1]])


def halve(block, bits, step):
    name, bit = step
    place = bits.index(step)
    mine = (lax.axis_index(name) >> bit) & 1
    sent = lax.dynamic_index_in_dim(block, 1 - mine, place, keepdims=False)
    kept = lax.dynamic_index_in_dim(block, mine, place, keepdims=False)
    pairs = [(i, i ^ (1 << bit)) for i in range(lax.axis_size(name))]
    got = lax.ppermute(sent, name, pairs)
    total = kept.astype(jnp.float32) + got.astype(jnp.float32)
    return (total, bits[:place] + bits[place + 1 :])


def halve_all(block, bits, order):
    total = block
    for step in order:
        total, bits = halve(total.astype(jnp.bfloat16), bits, step)
    return total


def block_scores(queries, key_block, block_idx, block_len, row_ids, doc_first):
    raw_scores = jnp.einsum(
        "qkgd,nkd->kgqn", queries, key_block, preferred_element_type=jnp.float32
    ) * HD ** (-0.5)
    columns = block_idx * block_len + jnp.arange(block_len, dtype=jnp.int32)
    allowed = (columns[None, :] <= row_ids[:, None]) & (columns[None, :] >= doc_first[:, None])
    return (jnp.where(allowed, raw_scores, masked_value), allowed)


def split_blocks(key_rows, value_rows):
    total_len = key_rows.shape[0]
    block_len = math.gcd(total_len, 1024)
    blocks = total_len // block_len
    key_tiles = key_rows.reshape(blocks, block_len, KVH, HD)
    value_tiles = value_rows.reshape(blocks, block_len, KVH, HD)
    indices = jnp.arange(blocks, dtype=jnp.int32)
    return (block_len, indices, key_tiles, value_tiles)


def attend_forward(queries, key_rows, value_rows, row_ids, doc_first):
    local_len, kv_heads, groups, head_dim = queries.shape
    block_len, indices, key_tiles, value_tiles = split_blocks(key_rows, value_rows)

    def first_pass(running, inputs):
        block_idx, key_block = inputs
        top_old, total_old = running
        masked, allowed = block_scores(queries, key_block, block_idx, block_len, row_ids, doc_first)
        top_new = jnp.maximum(top_old, jnp.max(masked, -1))
        exp_terms = jnp.where(allowed, jnp.exp(masked - top_new[..., None]), 0.0)
        return ((top_new, total_old * jnp.exp(top_old - top_new) + jnp.sum(exp_terms, -1)), None)

    start_top = jnp.full((kv_heads, groups, local_len), masked_value, jnp.float32)
    start_total = jnp.zeros((kv_heads, groups, local_len), jnp.float32)
    (row_top, row_total), _ = lax.scan(first_pass, (start_top, start_total), (indices, key_tiles))

    def second_pass(running, inputs):
        block_idx, key_block, value_block = inputs
        plain_sum, rest_sum = running
        masked, allowed = block_scores(queries, key_block, block_idx, block_len, row_ids, doc_first)
        prob_f = (
            jnp.where(allowed, jnp.exp(masked - row_top[..., None]), 0.0) / row_total[..., None]
        )
        prob_low = prob_f.astype(jnp.bfloat16)
        remainder = (prob_f - prob_low.astype(jnp.float32)).astype(jnp.bfloat16)
        plain_sum = plain_sum + jnp.einsum(
            "kgqn,nkd->qkgd", prob_low, value_block, preferred_element_type=jnp.float32
        )
        rest_sum = rest_sum + jnp.einsum(
            "kgqn,nkd->qkgd", remainder, value_block, preferred_element_type=jnp.float32
        )
        return ((plain_sum, rest_sum), None)

    zero_out = jnp.zeros((local_len, kv_heads, groups, head_dim), jnp.float32)
    (plain_sum, rest_sum), _ = lax.scan(
        second_pass, (zero_out, zero_out), (indices, key_tiles, value_tiles)
    )
    width = kv_heads * groups * head_dim
    return (
        row_top,
        row_total,
        plain_sum.reshape(local_len, width),
        (plain_sum + rest_sum).reshape(local_len, width),
    )


def attend_backward(
    queries, key_rows, value_rows, row_ids, doc_first, row_top, row_total, grad_out, row_delta
):
    local_len, kv_heads, groups, head_dim = queries.shape
    total_len = key_rows.shape[0]
    block_len, indices, key_tiles, value_tiles = split_blocks(key_rows, value_rows)
    scaling = HD ** (-0.5)

    def back_pass(running, inputs):
        block_idx, key_block, value_block = inputs
        masked, allowed = block_scores(queries, key_block, block_idx, block_len, row_ids, doc_first)
        prob_f = (
            jnp.where(allowed, jnp.exp(masked - row_top[..., None]), 0.0) / row_total[..., None]
        )
        prob_low = prob_f.astype(jnp.bfloat16)
        grad_prob = jnp.einsum(
            "qkgd,nkd->kgqn", grad_out, value_block, preferred_element_type=jnp.float32
        )
        grad_raw = (prob_f * (grad_prob - row_delta[..., None])).astype(jnp.bfloat16)
        new_q = (
            running
            + jnp.einsum("kgqn,nkd->qkgd", grad_raw, key_block, preferred_element_type=jnp.float32)
            * scaling
        )
        grad_k = (
            jnp.einsum("kgqn,qkgd->nkd", grad_raw, queries, preferred_element_type=jnp.float32)
            * scaling
        )
        grad_v = jnp.einsum(
            "kgqn,qkgd->nkd", prob_low, grad_out, preferred_element_type=jnp.float32
        )
        return (new_q, (grad_k, grad_v))

    zero_q = jnp.zeros((local_len, kv_heads, groups, head_dim), jnp.float32)
    grad_q, (grad_keys, grad_values) = lax.scan(
        back_pass, zero_q, (indices, key_tiles, value_tiles)
    )
    kv_width = kv_heads * head_dim
    grad_kv_rows = jnp.concatenate(
        [grad_keys.reshape(total_len, kv_width), grad_values.reshape(total_len, kv_width)], 1
    )
    return (grad_q.reshape(local_len, kv_heads * groups * head_dim), grad_kv_rows)


def on_device(
    hidden_in,
    doc_start,
    cotangent,
    attn_weight,
    gate_up,
    down_weight,
    gain_attn,
    gain_mlp,
    qkv_bias,
):
    stream = hidden_in[0].astype(jnp.float32)
    local_len = stream.shape[0]
    ctx_size = lax.axis_size("ctx")
    ctx_place = lax.axis_index("ctx")
    row_ids = ctx_place * local_len + jnp.arange(local_len, dtype=jnp.int32)
    doc_first = doc_start[0]
    cosine, sine_part = rope_tables(row_ids - doc_first)
    groups = HEADS // KVH
    weights = (
        lax.all_gather(attn_weight, ("dp", "ctx"), axis=0, tiled=True),
        lax.all_gather(gate_up, ("dp", "ctx"), axis=0, tiled=True),
        lax.all_gather(down_weight, ("dp", "ctx"), axis=0, tiled=True),
    )
    gain_len = D // ctx_size
    vectors = lax.all_gather(
        jnp.concatenate([gain_attn, gain_mlp, qkv_bias]), "ctx", axis=0, tiled=False
    ).astype(jnp.float32)
    attn_full, gate_full, down_full = weights
    gain_one = vectors[:, :gain_len].reshape(-1)
    gain_two = vectors[:, gain_len : 2 * gain_len].reshape(-1)
    bias_full = vectors[:, 2 * gain_len :].reshape(-1)
    factor_one = lax.rsqrt(jnp.mean(stream * stream, -1, keepdims=True) + epsilon)
    normed_one = (stream * factor_one * gain_one).astype(jnp.bfloat16)
    projected = contract_cols(normed_one, attn_full[:QKVD]) + bias_full
    queries = rotate(projected[:, :D].reshape(local_len, HEADS, HD), cosine, sine_part).astype(
        jnp.bfloat16
    )
    key_local = (
        rotate(projected[:, D : D + KVD].reshape(local_len, KVH, HD), cosine, sine_part)
        .astype(jnp.bfloat16)
        .reshape(local_len, KVD)
    )
    value_local = projected[:, D + KVD :].astype(jnp.bfloat16)
    kv_rows = lax.all_gather(
        jnp.concatenate([key_local, value_local], 1), "ctx", axis=0, tiled=True
    )
    key_rows, value_rows = kv_rows[:, :KVD], kv_rows[:, KVD:]
    grouped = queries.reshape(local_len, KVH, groups, HD)
    row_top, row_total, mixed_out, mixed_exact = attend_forward(
        grouped, key_rows, value_rows, row_ids, doc_first
    )
    mixed_low = mixed_out.astype(jnp.bfloat16)
    residual = stream + jnp.dot(mixed_low, attn_full[QKVD:], preferred_element_type=jnp.float32)
    factor_two = lax.rsqrt(jnp.mean(residual * residual, -1, keepdims=True) + epsilon)
    normed_two = (residual * factor_two * gain_two).astype(jnp.bfloat16)
    gate_up_act = contract_cols(normed_two, gate_full)
    gate_part = gate_up_act[:, :FF]
    up_part = gate_up_act[:, FF:]
    sigmoid_gate = jax.nn.sigmoid(gate_part)
    silu_gate = gate_part * sigmoid_gate
    activated = (silu_gate * up_part).astype(jnp.bfloat16)
    output = residual + jnp.dot(activated, down_full, preferred_element_type=jnp.float32)
    grad_two = cotangent[0]
    grad_stream = grad_two.astype(jnp.float32)
    grad_act = contract_cols(grad_two, down_full)
    grad_gate = grad_act * up_part * sigmoid_gate * (1.0 + gate_part * (1.0 - sigmoid_gate))
    grad_up = grad_act * silu_gate
    grad_gu = jnp.concatenate([grad_gate, grad_up], 1).astype(jnp.bfloat16)
    grad_normed = jnp.dot(grad_gu, gate_full, preferred_element_type=jnp.float32)
    gain_two_grad, grad_res = norm_back(grad_normed, residual, factor_two, gain_two)
    grad_mid = grad_stream + grad_res
    grad_mid_low = grad_mid.astype(jnp.bfloat16)
    grad_mixed = contract_cols(grad_mid_low, attn_full[QKVD:]).astype(jnp.bfloat16)
    grad_grouped = grad_mixed.reshape(local_len, KVH, groups, HD)
    exact_grouped = mixed_exact.reshape(local_len, KVH, groups, HD)
    row_delta = jnp.sum(grad_grouped.astype(jnp.float32) * exact_grouped, -1).transpose(1, 2, 0)
    grad_q, grad_kv_rows = attend_backward(
        grouped,
        key_rows,
        value_rows,
        row_ids,
        doc_first,
        row_top,
        row_total,
        grad_grouped,
        row_delta,
    )
    ctx_bits = index_bits("ctx")
    grad_kv = halve_all(split_bits(grad_kv_rows, ctx_bits), ctx_bits, ctx_bits[::-1])
    grad_q_raw = unrotate(grad_q.reshape(local_len, HEADS, HD), cosine, sine_part).reshape(
        local_len, D
    )
    grad_k_raw = unrotate(grad_kv[:, :KVD].reshape(local_len, KVH, HD), cosine, sine_part).reshape(
        local_len, KVD
    )
    grad_proj = jnp.concatenate([grad_q_raw, grad_k_raw, grad_kv[:, KVD:]], 1).astype(jnp.bfloat16)
    bias_grad = jnp.sum(grad_proj.astype(jnp.float32), 0)
    grad_normed_one = jnp.dot(grad_proj, attn_full[:QKVD], preferred_element_type=jnp.float32)
    gain_one_grad, grad_in = norm_back(grad_normed_one, stream, factor_one, gain_one)
    grad_input = grad_mid + grad_in
    dp_bits = index_bits("dp")
    all_bits = dp_bits + ctx_bits
    core, chip_bits = dp_bits[-1], dp_bits[:-1][::-1]
    ctx_up = ctx_bits[::-1]
    down_term = column_term(activated, grad_two).astype(jnp.bfloat16)
    down_sum = halve_all(
        split_bits(down_term, all_bits), all_bits, [core] + chip_bits + ctx_up
    )
    gate_term = column_term(grad_gu, normed_two).astype(jnp.bfloat16)
    gate_pair, pair_bits = halve(split_bits(gate_term, all_bits), all_bits, core)
    cut = gate_pair.shape[-2] // 2
    gate_pair = gate_pair.astype(jnp.bfloat16)
    gate_sum = jnp.concatenate(
        [
            halve_all(gate_pair[..., :cut, :], pair_bits, ctx_up + chip_bits),
            halve_all(gate_pair[..., cut:, :], pair_bits, ctx_bits + chip_bits),
        ],
        0,
    )
    attn_term = jnp.concatenate(
        [contract_rows(grad_proj, normed_one), contract_rows(mixed_low, grad_mid_low)], 0
    ).astype(jnp.bfloat16)
    attn_sum = halve_all(
        split_bits(attn_term, all_bits), all_bits, [core] + ctx_up + chip_bits
    )
    vector_terms = jnp.concatenate([gain_one_grad, gain_two_grad, bias_grad])
    gathered = jnp.sum(lax.all_gather(vector_terms, ("dp", "ctx"), axis=0, tiled=False), 0)
    vector_sums = (gathered[:D], gathered[D : 2 * D], gathered[2 * D :])
    bias_len = QKVD // ctx_size
    gain_one_part = lax.dynamic_slice_in_dim(vector_sums[0], ctx_place * gain_len, gain_len)
    gain_two_part = lax.dynamic_slice_in_dim(vector_sums[1], ctx_place * gain_len, gain_len)
    bias_part = lax.dynamic_slice_in_dim(vector_sums[2], ctx_place * bias_len, bias_len)
    return (
        output.astype(jnp.bfloat16)[None],
        grad_input.astype(jnp.bfloat16)[None],
        attn_sum,
        gate_sum,
        down_sum,
        gain_one_part,
        gain_two_part,
        bias_part,
    )


def solution(mesh):
    in_specs = (
        P("dp", "ctx", None),
        P("dp", "ctx"),
        P("dp", "ctx", None),
        P(("dp", "ctx"), None),
        P(("dp", "ctx"), None),
        P(("dp", "ctx"), None),
        P("ctx"),
        P("ctx"),
        P("ctx"),
    )
    out_specs = (
        P("dp", "ctx", None),
        P("dp", "ctx", None),
        P(("dp", "ctx"), None),
        P(("dp", "ctx"), None),
        P(("dp", "ctx"), None),
        P("ctx"),
        P("ctx"),
        P("ctx"),
    )
    return jax.shard_map(
        on_device, mesh=mesh, in_specs=in_specs, out_specs=out_specs, check_vma=False
    )
```

```python
import jax
import jax.numpy as jnp
from jax import lax
from jax.experimental import pallas as pl
from jax.experimental.pallas import tpu as pltpu
from jax.sharding import PartitionSpec as P

D = 896
HEADS = 14
KVH = 2
HD = 64
FF = 4864
KVD = 128
QKVD = 1152


epsilon = 1e-06
rope_base = 1000000.0
groups = HEADS // KVH
scaling = HD ** (-0.5)


def rope_tables(positions):
    half_dim = HD // 2
    frequency = rope_base ** (-jnp.arange(half_dim).astype(jnp.float32) * (2.0 / HD))
    angles = positions.astype(jnp.float32)[:, None] * frequency[None, :]
    return (jnp.cos(angles)[:, None, :], jnp.sin(angles)[:, None, :])


def rotate(values, cosine, sine_part):
    half_dim = values.shape[-1] // 2
    first_half = values[..., :half_dim]
    second_half = values[..., half_dim:]
    return jnp.concatenate(
        [
            first_half * cosine - second_half * sine_part,
            second_half * cosine + first_half * sine_part,
        ],
        -1,
    )


def unrotate(grad_in, cosine, sine_part):
    half_dim = grad_in.shape[-1] // 2
    first_half = grad_in[..., :half_dim]
    second_half = grad_in[..., half_dim:]
    return jnp.concatenate(
        [
            first_half * cosine + second_half * sine_part,
            second_half * cosine - first_half * sine_part,
        ],
        -1,
    )


def norm_back(grad_out, values, factor, gain_vec):
    scaled = grad_out * gain_vec
    gain_grad = jnp.sum(grad_out * values * factor, 0)
    inner_mean = jnp.mean(scaled * values, -1, keepdims=True)
    return (gain_grad, factor * scaled - values * factor**3 * inner_mean)


def contract_rows(left_op, right_op):
    return lax.dot_general(
        left_op, right_op, (((0,), (0,)), ((), ())), preferred_element_type=jnp.float32
    )


def contract_cols(left_op, right_op):
    return lax.dot_general(
        left_op, right_op, (((1,), (1,)), ((), ())), preferred_element_type=jnp.float32
    )


def column_term(left_op, right_op):
    return contract_rows(left_op, right_op)


def index_bits(axis_name):
    count = (lax.axis_size(axis_name) - 1).bit_length()
    return [(axis_name, bit) for bit in reversed(range(count))]


def split_bits(partial, bits):
    rows = partial.shape[0] >> len(bits)
    return partial.reshape([2] * len(bits) + [rows, partial.shape[1]])


def halve(block, bits, step):
    name, bit = step
    place = bits.index(step)
    mine = (lax.axis_index(name) >> bit) & 1
    sent = lax.dynamic_index_in_dim(block, 1 - mine, place, keepdims=False)
    kept = lax.dynamic_index_in_dim(block, mine, place, keepdims=False)
    pairs = [(i, i ^ (1 << bit)) for i in range(lax.axis_size(name))]
    got = lax.ppermute(sent, name, pairs)
    total = kept.astype(jnp.float32) + got.astype(jnp.float32)
    return (total, bits[:place] + bits[place + 1 :])


def halve_all(block, bits, order):
    total = block
    for step in order:
        total, bits = halve(total.astype(jnp.bfloat16), bits, step)
    return total


def partners(value, name):
    size = lax.axis_size(name)
    return [value] + [
        lax.ppermute(value, name, [(i, i ^ j) for i in range(size)]) for j in range(1, size)
    ]


def probabilities(keys, queries_t, cols, rows, first):
    scores = jnp.dot(keys, queries_t, preferred_element_type=jnp.float32) * scaling
    allowed = (cols <= rows) & (cols >= first)
    scores = jnp.where(allowed, scores, -jnp.inf)
    exp_terms = jnp.exp(scores - jnp.max(scores, 0, keepdims=True))
    return exp_terms * (1.0 / jnp.sum(exp_terms, 0, keepdims=True))


def forward_kernel(qt_ref, k_ref, vt_ref, col_ref, row_ref, first_ref, out_ref):
    prob = probabilities(k_ref[0], qt_ref[0], col_ref[...], row_ref[...], first_ref[...])
    out_ref[0] = jnp.dot(
        vt_ref[0], prob.astype(jnp.bfloat16), preferred_element_type=jnp.float32
    ).astype(jnp.bfloat16)


def backward_kernel(
    qt_ref, q_ref, gt_ref, g_ref, k_ref, kt_ref, v_ref, col_ref, row_ref, first_ref,
    dq_ref, dk_ref, dv_ref,
):
    @pl.when((pl.program_id(0) % groups == 0) & (pl.program_id(1) == 0))
    def _():
        dk_ref[...] = jnp.zeros_like(dk_ref)
        dv_ref[...] = jnp.zeros_like(dv_ref)

    prob = probabilities(k_ref[0], qt_ref[0], col_ref[...], row_ref[...], first_ref[...])
    grad_prob = jnp.dot(v_ref[0], gt_ref[0], preferred_element_type=jnp.float32)
    row_delta = jnp.sum(prob * grad_prob, 0, keepdims=True)
    grad_raw = (prob * (grad_prob - row_delta)).astype(jnp.bfloat16)
    dv_ref[0] += jnp.dot(prob.astype(jnp.bfloat16), g_ref[0], preferred_element_type=jnp.float32)
    dk_ref[0] += jnp.dot(grad_raw, q_ref[0], preferred_element_type=jnp.float32) * scaling
    dq_ref[0] = jnp.dot(kt_ref[0], grad_raw, preferred_element_type=jnp.float32) * scaling


def attention_specs(local_len, total_len):
    block = local_len if total_len <= 2048 or local_len % 128 else 128
    return (
        (HEADS, local_len // block),
        pl.BlockSpec((1, HD, block), lambda h, i: (h, 0, i)),
        pl.BlockSpec((1, block, HD), lambda h, i: (h, i, 0)),
        pl.BlockSpec((1, total_len, HD), lambda h, i: (h // groups, 0, 0)),
        pl.BlockSpec((1, HD, total_len), lambda h, i: (h // groups, 0, 0)),
        pl.BlockSpec((total_len, 1), lambda h, i: (0, 0)),
        pl.BlockSpec((1, block), lambda h, i: (0, i)),
    )


def attention_params(local_len, total_len, products):
    pairs = HEADS * local_len * total_len
    return dict(
        compiler_params=pltpu.CompilerParams(vmem_limit_bytes=48 * 1024 * 1024),
        cost_estimate=pl.CostEstimate(
            flops=2 * pairs * HD * products * 4, bytes_accessed=8 * 1024 * 1024, transcendentals=pairs
        ),
    )


def attend_forward(queries_t, keys, values_t, cols, rows, first):
    local_len, total_len = queries_t.shape[2], keys.shape[1]
    grid, wide, tall, key_rows, key_cols, col_spec, row_spec = attention_specs(local_len, total_len)
    return pl.pallas_call(
        forward_kernel,
        grid=grid,
        in_specs=[wide, key_rows, key_cols, col_spec, row_spec, row_spec],
        out_specs=wide,
        out_shape=jax.ShapeDtypeStruct((HEADS, HD, local_len), jnp.bfloat16),
        **attention_params(local_len, total_len, 2),
    )(queries_t, keys, values_t, cols, rows, first)


def attend_backward(queries_t, queries, grads_t, grads, keys, keys_t, values, cols, rows, first):
    local_len, total_len = queries_t.shape[2], keys.shape[1]
    grid, wide, tall, key_rows, key_cols, col_spec, row_spec = attention_specs(local_len, total_len)
    return pl.pallas_call(
        backward_kernel,
        grid=grid,
        in_specs=[wide, tall, wide, tall, key_rows, key_cols, key_rows]
        + [col_spec, row_spec, row_spec],
        out_specs=[wide, key_rows, key_rows],
        out_shape=[
            jax.ShapeDtypeStruct((HEADS, HD, local_len), jnp.float32),
            jax.ShapeDtypeStruct((KVH, total_len, HD), jnp.float32),
            jax.ShapeDtypeStruct((KVH, total_len, HD), jnp.float32),
        ],
        **attention_params(local_len, total_len, 5),
    )(queries_t, queries, grads_t, grads, keys, keys_t, values, cols, rows, first)


def on_device(
    hidden_in,
    doc_start,
    cotangent,
    attn_weight,
    gate_up,
    down_weight,
    gain_attn,
    gain_mlp,
    qkv_bias,
):
    stream = hidden_in[0].astype(jnp.float32)
    local_len = stream.shape[0]
    ctx_size = lax.axis_size("ctx")
    ctx_place = lax.axis_index("ctx")
    row_ids = ctx_place * local_len + jnp.arange(local_len, dtype=jnp.int32)
    doc_first = doc_start[0]
    cosine, sine_part = rope_tables(row_ids - doc_first)
    weights = (
        lax.all_gather(attn_weight, ("dp", "ctx"), axis=0, tiled=True),
        lax.all_gather(gate_up, ("dp", "ctx"), axis=0, tiled=True),
        lax.all_gather(down_weight, ("dp", "ctx"), axis=0, tiled=True),
    )
    gain_len = D // ctx_size
    places = jnp.arange(ctx_size, dtype=jnp.int32) ^ ctx_place
    vectors = jnp.stack(partners(jnp.concatenate([gain_attn, gain_mlp, qkv_bias]), "ctx"))
    vectors = jnp.take(vectors, places, axis=0).astype(jnp.float32)
    attn_full, gate_full, down_full = weights
    gain_one = vectors[:, :gain_len].reshape(-1)
    gain_two = vectors[:, gain_len : 2 * gain_len].reshape(-1)
    bias_full = vectors[:, 2 * gain_len :].reshape(-1)
    factor_one = lax.rsqrt(jnp.mean(stream * stream, -1, keepdims=True) + epsilon)
    normed_one = (stream * factor_one * gain_one).astype(jnp.bfloat16)
    projected = contract_cols(normed_one, attn_full[:QKVD]) + bias_full
    queries = rotate(projected[:, :D].reshape(local_len, HEADS, HD), cosine, sine_part).astype(
        jnp.bfloat16
    )
    key_local = (
        rotate(projected[:, D : D + KVD].reshape(local_len, KVH, HD), cosine, sine_part)
        .astype(jnp.bfloat16)
        .reshape(local_len, KVD)
    )
    value_local = projected[:, D + KVD :].astype(jnp.bfloat16)
    kv_rows = jnp.concatenate(
        partners(jnp.concatenate([key_local, value_local], 1), "ctx"), 0
    ).reshape(ctx_size * local_len, 2 * KVH, HD)
    kv_heads = kv_rows.transpose(1, 0, 2)
    kv_heads_t = kv_rows.transpose(1, 2, 0)
    cols = (places[:, None] * local_len + jnp.arange(local_len, dtype=jnp.int32)).reshape(-1, 1)
    place_args = (cols, row_ids[None, :], doc_first[None, :])
    queries_t = queries.transpose(1, 2, 0)
    mixed_t = attend_forward(queries_t, kv_heads[:KVH], kv_heads_t[KVH:], *place_args)
    mixed_low = mixed_t.transpose(2, 0, 1).reshape(local_len, D)
    residual = stream + jnp.dot(mixed_low, attn_full[QKVD:], preferred_element_type=jnp.float32)
    factor_two = lax.rsqrt(jnp.mean(residual * residual, -1, keepdims=True) + epsilon)
    normed_two = (residual * factor_two * gain_two).astype(jnp.bfloat16)
    gate_up_act = contract_cols(normed_two, gate_full)
    gate_part = gate_up_act[:, :FF]
    up_part = gate_up_act[:, FF:]
    sigmoid_gate = jax.nn.sigmoid(gate_part)
    silu_gate = gate_part * sigmoid_gate
    activated = (silu_gate * up_part).astype(jnp.bfloat16)
    output = residual + jnp.dot(activated, down_full, preferred_element_type=jnp.float32)
    grad_two = cotangent[0]
    grad_stream = grad_two.astype(jnp.float32)
    grad_act = contract_cols(grad_two, down_full)
    grad_gate = grad_act * up_part * sigmoid_gate * (1.0 + gate_part * (1.0 - sigmoid_gate))
    grad_up = grad_act * silu_gate
    grad_gu = jnp.concatenate([grad_gate, grad_up], 1).astype(jnp.bfloat16)
    grad_normed = jnp.dot(grad_gu, gate_full, preferred_element_type=jnp.float32)
    gain_two_grad, grad_res = norm_back(grad_normed, residual, factor_two, gain_two)
    grad_mid = grad_stream + grad_res
    grad_mid_low = grad_mid.astype(jnp.bfloat16)
    grad_mixed = contract_cols(grad_mid_low, attn_full[QKVD:]).astype(jnp.bfloat16)
    grad_heads = grad_mixed.reshape(local_len, HEADS, HD)
    grad_q_t, grad_keys, grad_values = attend_backward(
        queries_t,
        queries.transpose(1, 0, 2),
        grad_heads.transpose(1, 2, 0),
        grad_heads.transpose(1, 0, 2),
        kv_heads[:KVH],
        kv_heads_t[:KVH],
        kv_heads[KVH:],
        *place_args,
    )
    grad_q = grad_q_t.transpose(2, 0, 1)
    grad_kv_blocks = (
        jnp.concatenate([grad_keys, grad_values], 0)
        .astype(jnp.bfloat16)
        .reshape(2 * KVH, ctx_size, local_len, HD)
        .transpose(1, 2, 0, 3)
        .reshape(ctx_size, local_len, 2 * KVD)
    )
    grad_kv = grad_kv_blocks[0].astype(jnp.float32)
    for j in range(1, ctx_size):
        pairs = [(i, i ^ j) for i in range(ctx_size)]
        grad_kv = grad_kv + lax.ppermute(grad_kv_blocks[j], "ctx", pairs).astype(jnp.float32)
    ctx_bits = index_bits("ctx")
    grad_q_raw = unrotate(grad_q, cosine, sine_part).reshape(
        local_len, D
    )
    grad_k_raw = unrotate(grad_kv[:, :KVD].reshape(local_len, KVH, HD), cosine, sine_part).reshape(
        local_len, KVD
    )
    grad_proj = jnp.concatenate([grad_q_raw, grad_k_raw, grad_kv[:, KVD:]], 1).astype(jnp.bfloat16)
    bias_grad = jnp.sum(grad_proj.astype(jnp.float32), 0)
    grad_normed_one = jnp.dot(grad_proj, attn_full[:QKVD], preferred_element_type=jnp.float32)
    gain_one_grad, grad_in = norm_back(grad_normed_one, stream, factor_one, gain_one)
    grad_input = grad_mid + grad_in
    dp_bits = index_bits("dp")
    all_bits = dp_bits + ctx_bits
    core, chip_bits = dp_bits[-1], dp_bits[:-1][::-1]
    ctx_up = ctx_bits[::-1]
    down_term = column_term(activated, grad_two).astype(jnp.bfloat16)
    down_sum = halve_all(
        split_bits(down_term, all_bits), all_bits, [core] + chip_bits + ctx_up
    )
    gate_term = column_term(grad_gu, normed_two).astype(jnp.bfloat16)
    gate_pair, pair_bits = halve(split_bits(gate_term, all_bits), all_bits, core)
    cut = gate_pair.shape[-2] // 2
    gate_pair = gate_pair.astype(jnp.bfloat16)
    gate_sum = jnp.concatenate(
        [
            halve_all(gate_pair[..., :cut, :], pair_bits, ctx_up + chip_bits),
            halve_all(gate_pair[..., cut:, :], pair_bits, ctx_bits + chip_bits),
        ],
        0,
    )
    attn_term = jnp.concatenate(
        [contract_rows(grad_proj, normed_one), contract_rows(mixed_low, grad_mid_low)], 0
    ).astype(jnp.bfloat16)
    attn_sum = halve_all(
        split_bits(attn_term, all_bits), all_bits, [core] + ctx_up + chip_bits
    )
    bias_len = QKVD // ctx_size
    vector_sum = jnp.concatenate(
        [
            gain_one_grad.reshape(ctx_size, gain_len),
            gain_two_grad.reshape(ctx_size, gain_len),
            bias_grad.reshape(ctx_size, bias_len),
        ],
        1,
    ).reshape([2] * len(ctx_bits) + [2 * gain_len + bias_len])
    left = ctx_bits
    for step in ctx_up:
        vector_sum, left = halve(vector_sum, left, step)
    for name, bit in dp_bits[::-1]:
        pairs = [(i, i ^ (1 << bit)) for i in range(lax.axis_size(name))]
        vector_sum = vector_sum + lax.ppermute(vector_sum, name, pairs)
    gain_one_part = vector_sum[:gain_len]
    gain_two_part = vector_sum[gain_len : 2 * gain_len]
    bias_part = vector_sum[2 * gain_len :]
    return (
        output.astype(jnp.bfloat16)[None],
        grad_input.astype(jnp.bfloat16)[None],
        attn_sum,
        gate_sum,
        down_sum,
        gain_one_part,
        gain_two_part,
        bias_part,
    )


def solution(mesh):
    in_specs = (
        P("dp", "ctx", None),
        P("dp", "ctx"),
        P("dp", "ctx", None),
        P(("dp", "ctx"), None),
        P(("dp", "ctx"), None),
        P(("dp", "ctx"), None),
        P("ctx"),
        P("ctx"),
        P("ctx"),
    )
    out_specs = (
        P("dp", "ctx", None),
        P("dp", "ctx", None),
        P(("dp", "ctx"), None),
        P(("dp", "ctx"), None),
        P(("dp", "ctx"), None),
        P("ctx"),
        P("ctx"),
        P("ctx"),
    )
    return jax.shard_map(
        on_device, mesh=mesh, in_specs=in_specs, out_specs=out_specs, check_vma=False
    )
```

```python
import jax
import jax.numpy as jnp
from jax import lax
from jax.experimental import pallas as pl
from jax.experimental.pallas import tpu as pltpu
from jax.sharding import PartitionSpec as P

D = 896
HEADS = 14
KVH = 2
HD = 64
FF = 4864
KVD = 128
QKVD = 1152


epsilon = 1e-06
rope_base = 1000000.0
groups = HEADS // KVH
scaling = HD ** (-0.5)


def double(block, held, step, all_bits):
    name, bit = step
    pairs = [(i, i ^ (1 << bit)) for i in range(lax.axis_size(name))]
    got = lax.ppermute(block, name, pairs)
    held = [other for other in all_bits if other in held or other == step]
    is_low = (lax.axis_index(name) >> bit) & 1 == 0
    low, high = jnp.where(is_low, block, got), jnp.where(is_low, got, block)
    return (jnp.stack([low, high], held.index(step)), held)


def gather_halves(shard):
    dp_bits, ctx_bits = index_bits("dp"), index_bits("ctx")
    all_bits = dp_bits + ctx_bits
    cut = shard.shape[0] // 2
    halves = []
    for part, ctx_order in ((shard[:cut], ctx_bits), (shard[cut:], ctx_bits[::-1])):
        held = []
        for step in dp_bits[:-1] + ctx_order:
            part, held = double(part, held, step, all_bits)
        halves.append(part)
    full, held = double(jnp.concatenate(halves, -2), held, dp_bits[-1], all_bits)
    return full.reshape(-1, shard.shape[1])


def rope_tables(positions):
    half_dim = HD // 2
    frequency = rope_base ** (-jnp.arange(half_dim).astype(jnp.float32) * (2.0 / HD))
    angles = positions.astype(jnp.float32)[:, None] * frequency[None, :]
    return (jnp.cos(angles)[:, None, :], jnp.sin(angles)[:, None, :])


def rotate(values, cosine, sine_part):
    half_dim = values.shape[-1] // 2
    first_half = values[..., :half_dim]
    second_half = values[..., half_dim:]
    return jnp.concatenate(
        [
            first_half * cosine - second_half * sine_part,
            second_half * cosine + first_half * sine_part,
        ],
        -1,
    )


def unrotate(grad_in, cosine, sine_part):
    half_dim = grad_in.shape[-1] // 2
    first_half = grad_in[..., :half_dim]
    second_half = grad_in[..., half_dim:]
    return jnp.concatenate(
        [
            first_half * cosine + second_half * sine_part,
            second_half * cosine - first_half * sine_part,
        ],
        -1,
    )


def norm_back(grad_out, values, factor, gain_vec):
    scaled = grad_out * gain_vec
    gain_grad = jnp.sum(grad_out * values * factor, 0)
    inner_mean = jnp.mean(scaled * values, -1, keepdims=True)
    return (gain_grad, factor * scaled - values * factor**3 * inner_mean)


def contract_rows(left_op, right_op):
    return lax.dot_general(
        left_op, right_op, (((0,), (0,)), ((), ())), preferred_element_type=jnp.float32
    )


def contract_cols(left_op, right_op):
    return lax.dot_general(
        left_op, right_op, (((1,), (1,)), ((), ())), preferred_element_type=jnp.float32
    )


def column_term(left_op, right_op):
    return contract_rows(left_op, right_op)


def index_bits(axis_name):
    count = (lax.axis_size(axis_name) - 1).bit_length()
    return [(axis_name, bit) for bit in reversed(range(count))]


def split_bits(partial, bits):
    rows = partial.shape[0] >> len(bits)
    return partial.reshape([2] * len(bits) + [rows, partial.shape[1]])


def halve(block, bits, step):
    name, bit = step
    place = bits.index(step)
    mine = (lax.axis_index(name) >> bit) & 1
    sent = lax.dynamic_index_in_dim(block, 1 - mine, place, keepdims=False)
    kept = lax.dynamic_index_in_dim(block, mine, place, keepdims=False)
    pairs = [(i, i ^ (1 << bit)) for i in range(lax.axis_size(name))]
    got = lax.ppermute(sent, name, pairs)
    total = kept.astype(jnp.float32) + got.astype(jnp.float32)
    return (total, bits[:place] + bits[place + 1 :])


def halve_all(block, bits, order):
    total = block
    for step in order:
        total, bits = halve(total.astype(jnp.bfloat16), bits, step)
    return total


def partners(value, name):
    size = lax.axis_size(name)
    return [value] + [
        lax.ppermute(value, name, [(i, i ^ j) for i in range(size)]) for j in range(1, size)
    ]


def probabilities(keys, queries_t, cols, rows, first):
    scores = jnp.dot(keys, queries_t, preferred_element_type=jnp.float32) * scaling
    allowed = (cols <= rows) & (cols >= first)
    scores = jnp.where(allowed, scores, -jnp.inf)
    exp_terms = jnp.exp(scores - jnp.max(scores, 0, keepdims=True))
    return exp_terms * (1.0 / jnp.sum(exp_terms, 0, keepdims=True))


def forward_kernel(qt_ref, k_ref, vt_ref, col_ref, row_ref, first_ref, out_ref):
    prob = probabilities(k_ref[0], qt_ref[0], col_ref[...], row_ref[...], first_ref[...])
    out_ref[0] = jnp.dot(
        vt_ref[0], prob.astype(jnp.bfloat16), preferred_element_type=jnp.float32
    ).astype(jnp.bfloat16)


def backward_kernel(
    qt_ref, q_ref, gt_ref, g_ref, k_ref, kt_ref, v_ref, col_ref, row_ref, first_ref,
    dq_ref, dk_ref, dv_ref,
):
    @pl.when((pl.program_id(0) % groups == 0) & (pl.program_id(1) == 0))
    def _():
        dk_ref[...] = jnp.zeros_like(dk_ref)
        dv_ref[...] = jnp.zeros_like(dv_ref)

    prob = probabilities(k_ref[0], qt_ref[0], col_ref[...], row_ref[...], first_ref[...])
    grad_prob = jnp.dot(v_ref[0], gt_ref[0], preferred_element_type=jnp.float32)
    row_delta = jnp.sum(prob * grad_prob, 0, keepdims=True)
    grad_raw = (prob * (grad_prob - row_delta)).astype(jnp.bfloat16)
    dv_ref[0] += jnp.dot(prob.astype(jnp.bfloat16), g_ref[0], preferred_element_type=jnp.float32)
    dk_ref[0] += jnp.dot(grad_raw, q_ref[0], preferred_element_type=jnp.float32) * scaling
    dq_ref[0] = jnp.dot(kt_ref[0], grad_raw, preferred_element_type=jnp.float32) * scaling


def attention_specs(local_len, total_len):
    block = local_len if total_len <= 2048 or local_len % 128 else 128
    return (
        (HEADS, local_len // block),
        pl.BlockSpec((1, HD, block), lambda h, i: (h, 0, i)),
        pl.BlockSpec((1, block, HD), lambda h, i: (h, i, 0)),
        pl.BlockSpec((1, total_len, HD), lambda h, i: (h // groups, 0, 0)),
        pl.BlockSpec((1, HD, total_len), lambda h, i: (h // groups, 0, 0)),
        pl.BlockSpec((total_len, 1), lambda h, i: (0, 0)),
        pl.BlockSpec((1, block), lambda h, i: (0, i)),
    )


def attention_params(local_len, total_len, products):
    pairs = HEADS * local_len * total_len
    return dict(
        compiler_params=pltpu.CompilerParams(vmem_limit_bytes=48 * 1024 * 1024),
        cost_estimate=pl.CostEstimate(
            flops=2 * pairs * HD * products * 4, bytes_accessed=8 * 1024 * 1024, transcendentals=pairs
        ),
    )


def attend_forward(queries_t, keys, values_t, cols, rows, first):
    local_len, total_len = queries_t.shape[2], keys.shape[1]
    grid, wide, tall, key_rows, key_cols, col_spec, row_spec = attention_specs(local_len, total_len)
    return pl.pallas_call(
        forward_kernel,
        grid=grid,
        in_specs=[wide, key_rows, key_cols, col_spec, row_spec, row_spec],
        out_specs=wide,
        out_shape=jax.ShapeDtypeStruct((HEADS, HD, local_len), jnp.bfloat16),
        **attention_params(local_len, total_len, 2),
    )(queries_t, keys, values_t, cols, rows, first)


def attend_backward(queries_t, queries, grads_t, grads, keys, keys_t, values, cols, rows, first):
    local_len, total_len = queries_t.shape[2], keys.shape[1]
    grid, wide, tall, key_rows, key_cols, col_spec, row_spec = attention_specs(local_len, total_len)
    return pl.pallas_call(
        backward_kernel,
        grid=grid,
        in_specs=[wide, tall, wide, tall, key_rows, key_cols, key_rows]
        + [col_spec, row_spec, row_spec],
        out_specs=[wide, key_rows, key_rows],
        out_shape=[
            jax.ShapeDtypeStruct((HEADS, HD, local_len), jnp.float32),
            jax.ShapeDtypeStruct((KVH, total_len, HD), jnp.float32),
            jax.ShapeDtypeStruct((KVH, total_len, HD), jnp.float32),
        ],
        **attention_params(local_len, total_len, 5),
    )(queries_t, queries, grads_t, grads, keys, keys_t, values, cols, rows, first)


def on_device(
    hidden_in,
    doc_start,
    cotangent,
    attn_weight,
    gate_up,
    down_weight,
    gain_attn,
    gain_mlp,
    qkv_bias,
):
    stream = hidden_in[0].astype(jnp.float32)
    local_len = stream.shape[0]
    ctx_size = lax.axis_size("ctx")
    ctx_place = lax.axis_index("ctx")
    row_ids = ctx_place * local_len + jnp.arange(local_len, dtype=jnp.int32)
    doc_first = doc_start[0]
    cosine, sine_part = rope_tables(row_ids - doc_first)
    weights = (
        lax.all_gather(attn_weight, ("dp", "ctx"), axis=0, tiled=True),
        gather_halves(gate_up),
        lax.all_gather(down_weight, ("dp", "ctx"), axis=0, tiled=True),
    )
    gain_len = D // ctx_size
    places = jnp.arange(ctx_size, dtype=jnp.int32) ^ ctx_place
    vectors = jnp.stack(partners(jnp.concatenate([gain_attn, gain_mlp, qkv_bias]), "ctx"))
    vectors = jnp.take(vectors, places, axis=0).astype(jnp.float32)
    attn_full, gate_full, down_full = weights
    gain_one = vectors[:, :gain_len].reshape(-1)
    gain_two = vectors[:, gain_len : 2 * gain_len].reshape(-1)
    bias_full = vectors[:, 2 * gain_len :].reshape(-1)
    factor_one = lax.rsqrt(jnp.mean(stream * stream, -1, keepdims=True) + epsilon)
    normed_one = (stream * factor_one * gain_one).astype(jnp.bfloat16)
    projected = contract_cols(normed_one, attn_full[:QKVD]) + bias_full
    queries = rotate(projected[:, :D].reshape(local_len, HEADS, HD), cosine, sine_part).astype(
        jnp.bfloat16
    )
    key_local = (
        rotate(projected[:, D : D + KVD].reshape(local_len, KVH, HD), cosine, sine_part)
        .astype(jnp.bfloat16)
        .reshape(local_len, KVD)
    )
    value_local = projected[:, D + KVD :].astype(jnp.bfloat16)
    kv_rows = jnp.concatenate(
        partners(jnp.concatenate([key_local, value_local], 1), "ctx"), 0
    ).reshape(ctx_size * local_len, 2 * KVH, HD)
    kv_heads = kv_rows.transpose(1, 0, 2)
    kv_heads_t = kv_rows.transpose(1, 2, 0)
    cols = (places[:, None] * local_len + jnp.arange(local_len, dtype=jnp.int32)).reshape(-1, 1)
    place_args = (cols, row_ids[None, :], doc_first[None, :])
    queries_t = queries.transpose(1, 2, 0)
    mixed_t = attend_forward(queries_t, kv_heads[:KVH], kv_heads_t[KVH:], *place_args)
    mixed_low = mixed_t.transpose(2, 0, 1).reshape(local_len, D)
    residual = stream + jnp.dot(mixed_low, attn_full[QKVD:], preferred_element_type=jnp.float32)
    factor_two = lax.rsqrt(jnp.mean(residual * residual, -1, keepdims=True) + epsilon)
    normed_two = (residual * factor_two * gain_two).astype(jnp.bfloat16)
    gate_up_act = contract_cols(normed_two, gate_full)
    gate_part = gate_up_act[:, :FF]
    up_part = gate_up_act[:, FF:]
    sigmoid_gate = jax.nn.sigmoid(gate_part)
    silu_gate = gate_part * sigmoid_gate
    activated = (silu_gate * up_part).astype(jnp.bfloat16)
    output = residual + jnp.dot(activated, down_full, preferred_element_type=jnp.float32)
    grad_two = cotangent[0]
    grad_stream = grad_two.astype(jnp.float32)
    grad_act = contract_cols(grad_two, down_full)
    grad_gate = grad_act * up_part * sigmoid_gate * (1.0 + gate_part * (1.0 - sigmoid_gate))
    grad_up = grad_act * silu_gate
    grad_gu = jnp.concatenate([grad_gate, grad_up], 1).astype(jnp.bfloat16)
    grad_normed = jnp.dot(grad_gu, gate_full, preferred_element_type=jnp.float32)
    gain_two_grad, grad_res = norm_back(grad_normed, residual, factor_two, gain_two)
    grad_mid = grad_stream + grad_res
    grad_mid_low = grad_mid.astype(jnp.bfloat16)
    grad_mixed = contract_cols(grad_mid_low, attn_full[QKVD:]).astype(jnp.bfloat16)
    grad_heads = grad_mixed.reshape(local_len, HEADS, HD)
    grad_q_t, grad_keys, grad_values = attend_backward(
        queries_t,
        queries.transpose(1, 0, 2),
        grad_heads.transpose(1, 2, 0),
        grad_heads.transpose(1, 0, 2),
        kv_heads[:KVH],
        kv_heads_t[:KVH],
        kv_heads[KVH:],
        *place_args,
    )
    grad_q = grad_q_t.transpose(2, 0, 1)
    grad_kv_blocks = (
        jnp.concatenate([grad_keys, grad_values], 0)
        .astype(jnp.bfloat16)
        .reshape(2 * KVH, ctx_size, local_len, HD)
        .transpose(1, 2, 0, 3)
        .reshape(ctx_size, local_len, 2 * KVD)
    )
    grad_kv = grad_kv_blocks[0].astype(jnp.float32)
    for j in range(1, ctx_size):
        pairs = [(i, i ^ j) for i in range(ctx_size)]
        grad_kv = grad_kv + lax.ppermute(grad_kv_blocks[j], "ctx", pairs).astype(jnp.float32)
    ctx_bits = index_bits("ctx")
    grad_q_raw = unrotate(grad_q, cosine, sine_part).reshape(
        local_len, D
    )
    grad_k_raw = unrotate(grad_kv[:, :KVD].reshape(local_len, KVH, HD), cosine, sine_part).reshape(
        local_len, KVD
    )
    grad_proj = jnp.concatenate([grad_q_raw, grad_k_raw, grad_kv[:, KVD:]], 1).astype(jnp.bfloat16)
    bias_grad = jnp.sum(grad_proj.astype(jnp.float32), 0)
    grad_normed_one = jnp.dot(grad_proj, attn_full[:QKVD], preferred_element_type=jnp.float32)
    gain_one_grad, grad_in = norm_back(grad_normed_one, stream, factor_one, gain_one)
    grad_input = grad_mid + grad_in
    dp_bits = index_bits("dp")
    all_bits = dp_bits + ctx_bits
    core, chip_bits = dp_bits[-1], dp_bits[:-1][::-1]
    ctx_up = ctx_bits[::-1]
    down_term = column_term(activated, grad_two).astype(jnp.bfloat16)
    down_sum = halve_all(
        split_bits(down_term, all_bits), all_bits, [core] + chip_bits + ctx_up
    )
    gate_term = column_term(grad_gu, normed_two).astype(jnp.bfloat16)
    gate_pair, pair_bits = halve(split_bits(gate_term, all_bits), all_bits, core)
    cut = gate_pair.shape[-2] // 2
    gate_pair = gate_pair.astype(jnp.bfloat16)
    gate_sum = jnp.concatenate(
        [
            halve_all(gate_pair[..., :cut, :], pair_bits, ctx_up + chip_bits),
            halve_all(gate_pair[..., cut:, :], pair_bits, ctx_bits + chip_bits),
        ],
        0,
    )
    attn_term = jnp.concatenate(
        [contract_rows(grad_proj, normed_one), contract_rows(mixed_low, grad_mid_low)], 0
    ).astype(jnp.bfloat16)
    attn_sum = halve_all(
        split_bits(attn_term, all_bits), all_bits, [core] + ctx_up + chip_bits
    )
    bias_len = QKVD // ctx_size
    vector_sum = jnp.concatenate(
        [
            gain_one_grad.reshape(ctx_size, gain_len),
            gain_two_grad.reshape(ctx_size, gain_len),
            bias_grad.reshape(ctx_size, bias_len),
        ],
        1,
    ).reshape([2] * len(ctx_bits) + [2 * gain_len + bias_len])
    left = ctx_bits
    for step in ctx_up:
        vector_sum, left = halve(vector_sum, left, step)
    for name, bit in dp_bits[::-1]:
        pairs = [(i, i ^ (1 << bit)) for i in range(lax.axis_size(name))]
        vector_sum = vector_sum + lax.ppermute(vector_sum, name, pairs)
    gain_one_part = vector_sum[:gain_len]
    gain_two_part = vector_sum[gain_len : 2 * gain_len]
    bias_part = vector_sum[2 * gain_len :]
    return (
        output.astype(jnp.bfloat16)[None],
        grad_input.astype(jnp.bfloat16)[None],
        attn_sum,
        gate_sum,
        down_sum,
        gain_one_part,
        gain_two_part,
        bias_part,
    )


def solution(mesh):
    in_specs = (
        P("dp", "ctx", None),
        P("dp", "ctx"),
        P("dp", "ctx", None),
        P(("dp", "ctx"), None),
        P(("dp", "ctx"), None),
        P(("dp", "ctx"), None),
        P("ctx"),
        P("ctx"),
        P("ctx"),
    )
    out_specs = (
        P("dp", "ctx", None),
        P("dp", "ctx", None),
        P(("dp", "ctx"), None),
        P(("dp", "ctx"), None),
        P(("dp", "ctx"), None),
        P("ctx"),
        P("ctx"),
        P("ctx"),
    )
    return jax.shard_map(
        on_device, mesh=mesh, in_specs=in_specs, out_specs=out_specs, check_vma=False
    )
```
